512 devices in a mesh: space: 64 (over x, z, core), snap: 8 (over y).
Axes of the slice: x: 4, y: 8, z: 8, core: 2. Of those that a mesh axis runs over, the one named last changes fastest.
Arguments:
- snapshots: bfloat16 [32768, 3, 1024], P('space', None, 'snap'), may hold values from -16 to 16
- mass_blocks: bfloat16 [512, 7, 4096], P('space'), may hold values from -0.25 to 0.25
- block_cols: int32 [512, 7], P('space'), may hold values from 0 to 511, as said below
- coefficients: bfloat16 [1024, 64], P('snap'), may hold values from -0.1875 to 0.1875
- lumped: float32 [32768], P('space'), may hold values from 0.3 to 9
Outputs:
- gram: float32 [1024, 1024], P('snap', 'space')
- modes: bfloat16 [32768, 3, 64], P('space')
The draws below stay inside these ranges and needn't reach their ends.
Inputs may be any that keep to these rules, and one draw needn't show every extreme that they name: `block_cols`: entries 0, 1, 2 of row b are b, b - 1, b + 1 (b itself where that block does not exist); every entry lies within 3 blocks of its row; entries may repeat.
All inputs are finite; a program needn't handle non-finite values.
Results may differ from the reference program's by a relative error of at most 0.0029.
Values may be sent and summed in bfloat16 or wider, within the bound.
No kernel may reach another device: no remote copies, remote signals or barrier semaphores. Data moves between devices by JAX's collectives and lax.ppermute only.
A program may use at most 128 MiB of HBM per device.

```python
import jax
import jax.numpy as jnp
from jax import lax

BLOCK = 64
BPR = 7
REACH = 3
NBD = 8
NMODES = 64
NBLK = 512
NODES = 32768
NSNAP = 1024
N_SPACE = 64


def draw_block_cols(key, part):
    key = jax.random.fold_in(key, 11)
    block_rows = jnp.arange(NBLK, dtype=jnp.int32)[:, None]
    extra = jax.random.randint(key, (NBLK, BPR - 3), -REACH, REACH + 1, dtype=jnp.int32)
    fixed_steps = jnp.broadcast_to(jnp.array([0, -1, 1], dtype=jnp.int32), (NBLK, 3))
    targets = block_rows + jnp.concatenate([fixed_steps, extra], axis=1)
    outside = (targets < 0) | (targets >= NBLK)
    return jnp.where(outside, jnp.broadcast_to(block_rows, targets.shape), targets).astype(jnp.int32)


def draw_lumped(key, part):
    key = jax.random.fold_in(key, 5)
    spread = jnp.exp(jax.random.uniform(key, (NODES,), jnp.float32, jnp.log(0.3), jnp.log(3.0)))
    ramp = jnp.exp(jnp.log(3.0) * jnp.arange(NODES, dtype=jnp.float32) / NODES)
    return spread * ramp


def strengthened(entries, own_key, source, target, blocks, factor):
    owner, partner = [(jnp.arange(entries.shape[dim]) // (entries.shape[dim] // blocks)).reshape([-1 if axis == dim else 1 for axis in range(entries.ndim)]) for dim in (source, target)]
    chosen = jax.random.permutation(own_key, blocks)[partner]
    strong = (owner == chosen) | (owner == (partner + blocks // 2) % blocks)
    return jnp.where(strong, factor * entries, entries)


def levels(stream_key, extent, split, low, high):
    gain, own = 1.0, jax.random.fold_in(stream_key, 6)
    for position, parts in split:
        steps = jnp.exp(jax.random.uniform(jax.random.fold_in(own, position), (parts,), jnp.float32, low / len(split), high / len(split)))
        gain = gain * jnp.repeat(steps, extent[position] // parts).reshape([-1 if axis == position else 1 for axis in range(len(extent))])
    return gain


def gaussian(rng, dims, scale, bound, split=(), kind=jnp.bfloat16):
    entries = scale * jax.random.normal(rng, dims, jnp.float32)
    if split:
        entries = entries * levels(rng, dims, split, -0.22, 0.18)
    return jnp.clip(entries, -bound, bound).astype(kind)


def noise_with(stream_key, extent, scale, bound, shards, heavy, kind=jnp.bfloat16):
    values = scale * jax.random.normal(stream_key, extent, jnp.float32)
    if shards:
        values = values * levels(stream_key, extent, shards, -0.22, 0.18)
    return jnp.clip(strengthened(values, jax.random.fold_in(stream_key, 3), *heavy), -bound, bound).astype(kind)


def setup_inputs(seed: int = 0) -> dict:
    keys = jax.random.split(jax.random.key(seed), 6)
    snapshots = noise_with(keys[0], (NODES, 3, NSNAP), 1.0, 16.0, ((0, 64), (2, 8)), (0, 2, 64, 4.0))
    mass_blocks = gaussian(keys[1], (NBLK, BPR, BLOCK * BLOCK), (BLOCK * BPR) ** -0.5, 0.25, ((0, 64),))
    block_cols = draw_block_cols(jax.random.fold_in(keys[5], 71), 0)
    coefficients = gaussian(keys[3], (NSNAP, NMODES), NSNAP ** -0.5, 0.1875, ((0, 8),))
    lumped = draw_lumped(jax.random.fold_in(keys[5], 71), 0)
    return {"snapshots": snapshots, "mass_blocks": mass_blocks, "block_cols": block_cols, "coefficients": coefficients, "lumped": lumped}


def reference(snapshots, mass_blocks, block_cols, coefficients, lumped):
    columns = 3 * NSNAP
    blocks = snapshots.reshape(NBLK, BLOCK, columns)
    weights = coefficients.astype(jnp.float32)
    square_mass = mass_blocks.reshape(NBLK, BPR, BLOCK, BLOCK)

    def slab_step(total, slab):
        start = (slab * NBD).astype(jnp.int32)
        slab_rows = lax.dynamic_slice_in_dim(blocks, start, NBD, 0)
        slab_cols = lax.dynamic_slice_in_dim(block_cols, start, NBD, 0)
        slab_mass = lax.dynamic_slice_in_dim(square_mass, start, NBD, 0)
        near_blocks = jnp.take(blocks, slab_cols, axis=0)
        mass_image = jnp.einsum('bjnm,bjmw->bnw', slab_mass.astype(jnp.float32), near_blocks.astype(jnp.float32), precision=lax.Precision.HIGHEST).astype(jnp.bfloat16)
        left_side = slab_rows.reshape(NBD * BLOCK, 3, NSNAP).astype(jnp.float32)
        right_side = mass_image.reshape(NBD * BLOCK, 3, NSNAP).astype(jnp.float32)
        total = total + jnp.einsum('nca,ncb->ab', left_side, right_side, precision=lax.Precision.HIGHEST)
        mode_terms = jnp.einsum('nca,ak->nck', left_side, weights, precision=lax.Precision.HIGHEST)
        return (total, mode_terms)
    total, mode_terms = lax.scan(slab_step, jnp.zeros((NSNAP, NSNAP), jnp.float32), jnp.arange(N_SPACE, dtype=jnp.int32))
    gram = total * (3.0 * NODES) ** (-0.5)
    raw_modes = mode_terms.reshape(NODES, 3, NMODES)
    norm_sums = lax.optimization_barrier(jnp.sum(lumped[:, None, None] * raw_modes * raw_modes, axis=(0, 1))) / (3.0 * NODES)
    modes = (raw_modes * lax.rsqrt(norm_sums + 1e-06)).astype(jnp.bfloat16)
    return (gram, modes)
```

```python
import jax
import jax.numpy as jnp
from jax import lax
from jax.experimental import pallas as pl
from jax.experimental.pallas import tpu as pltpu
from jax.sharding import Mesh, PartitionSpec as P

BLOCK = 64
BPR = 7
REACH = 3
NX, NZ, NC, NY = 4, 8, 2, 8
ROWS = 3 * BLOCK
MODES = 64
TILE = 128
NROW = 16
F32 = jnp.float32
BF16 = jnp.bfloat16
SPACE = ("x", "z", "core")


def image_kernel(cols, mass, own, low, high, out, ext):
    blocks = own.shape[1] // BLOCK
    index = (lax.axis_index("x") * NZ + lax.axis_index("z")) * NC + lax.axis_index("core")
    first = index * blocks - REACH
    for c in range(3):
        lanes = pl.ds(c * TILE, TILE)
        ext[:REACH, :, lanes] = low[c].reshape(REACH, BLOCK, TILE)
        ext[REACH : REACH + blocks, :, lanes] = own[c].reshape(blocks, BLOCK, TILE)
        ext[REACH + blocks :, :, lanes] = high[c].reshape(REACH, BLOCK, TILE)
    for b in range(blocks):
        near = jnp.concatenate([ext[cols[b, j] - first] for j in range(BPR)], axis=0)
        total = jnp.dot(mass[b], near, preferred_element_type=F32).astype(BF16)
        for c in range(3):
            out[b, c * BLOCK : (c + 1) * BLOCK, :] = total[:, c * TILE : (c + 1) * TILE]


def raw_kernel(snaps, lumped, raw_out, norm_out):
    raw = jnp.zeros((MODES, ROWS), F32)
    for t in range(NY):
        raw = raw + lax.dot_general(
            snaps[t, ROWS:, :], snaps[t, :ROWS, :], (((1,), (1,)), ((), ())), preferred_element_type=F32
        )
    column = jnp.zeros((MODES, 1), F32)
    for c in range(3):
        part = raw[:, c * BLOCK : (c + 1) * BLOCK]
        column = column + jnp.sum(lumped[...] * part * part, axis=1, keepdims=True)
        raw_out[c * 32 : (c + 1) * 32, :] = jnp.concatenate([part[:32], part[32:]], axis=1)
    k = lax.broadcasted_iota(jnp.int32, (MODES, TILE), 0)
    lane = lax.broadcasted_iota(jnp.int32, (MODES, TILE), 1)
    row = jnp.sum(jnp.where(lane % MODES == k, column, 0.0), axis=0, keepdims=True)
    norm_out[...] = split_row(row, NROW)


def split_row(row, count):
    high = row.astype(BF16)
    rest = (row - high.astype(F32)).astype(BF16)
    lane = lax.broadcasted_iota(jnp.int32, (1, TILE), 1)
    both = jnp.where(lane < MODES, high.astype(F32), rest.astype(F32))
    return jnp.broadcast_to(both, (count, TILE)).astype(BF16)


def join_row(row):
    return row + pltpu.roll(row, MODES, 1)


def gram_kernel(snaps, other_snaps, image, other_image, norm, out):
    core = lax.axis_index("core")
    half = NY // NC
    mine = [snaps[core * half + q, :ROWS, :] for q in range(half)]
    right = jnp.concatenate(
        [jnp.concatenate(mine, axis=1), jnp.concatenate([other_snaps[q] for q in range(half)], axis=1)], axis=0
    )
    per = NY // NX
    for t in range(NY):
        left = jnp.concatenate([image[t], other_image[t]], axis=0)
        tile = lax.dot_general(left, right, (((0,), (0,)), ((), ())), preferred_element_type=F32).astype(BF16)
        for q in range(half):
            base = q * per * TILE + (t % per) * TILE
            out[t // per, base : base + TILE, :] = tile[:, q * TILE : (q + 1) * TILE]
    for x in range(NX):
        out[x, half * per * TILE :, :] = norm[...]


def sum_x_kernel(parts, out):
    half = NY // NC
    per = 32
    total = parts[0].astype(F32)
    for x in range(1, NX):
        total = total + parts[x].astype(F32)
    rows = half * NZ * per
    for q in range(half):
        for z in range(NZ):
            base = (q * NZ + z) * per
            out[z, q * per : (q + 1) * per, :] = total[base : base + per].astype(BF16)
    row = split_row(join_row(total[rows : rows + 1]), NROW)
    for z in range(NZ):
        out[z, half * per :, :] = row


def sum_z_kernel(parts, out):
    core = lax.axis_index("core")
    half = NY // NC
    per = 32
    total = parts[0].astype(F32)
    for z in range(1, NZ):
        total = total + parts[z].astype(F32)
    rows = half * per
    row = jnp.broadcast_to(join_row(total[rows : rows + 1]), (8, TILE))
    for c in range(NC):
        for q in range(half):
            base = q * per + c * 16
            out[c * NY + core * half + q, :16, :] = total[base : base + 16]
            out[c * NY + (1 - core) * half + q, :16, :] = jnp.zeros((16, TILE), F32)
    for i in range(NC * NY):
        out[i, 16:, :] = row


def final_kernel(nodes, parts, raw, gram, modes):
    total = parts[0]
    for i in range(1, NC * NY):
        total = total + parts[i]
    gram[...] = total[:16] * (3.0 * nodes) ** (-0.5)
    row = lax.rsqrt(total[16:17] / (3.0 * nodes) + 1e-06)
    k = lax.broadcasted_iota(jnp.int32, (MODES, TILE), 0)
    lane = lax.broadcasted_iota(jnp.int32, (MODES, TILE), 1)
    column = jnp.sum(jnp.where(lane == k, row, 0.0), axis=1, keepdims=True)
    low, high = column[:32], column[32:]
    for c in range(3):
        rows = slice(c * 32, (c + 1) * 32)
        for u in range(NY // 2):
            a, b = raw[2 * u, rows, :], raw[2 * u + 1, rows, :]
            lanes = slice(u * TILE, (u + 1) * TILE)
            first = jnp.concatenate([a[:, :MODES], b[:, :MODES]], axis=1)
            second = jnp.concatenate([a[:, MODES:], b[:, MODES:]], axis=1)
            modes[c, :32, lanes] = (first * low).astype(BF16)
            modes[c, 32:, lanes] = (second * high).astype(BF16)


def call(kernel, shapes, *args, scratch=(), smem=0):
    specs = [pl.BlockSpec(memory_space=pltpu.SMEM)] * smem
    specs += [pl.BlockSpec(memory_space=pltpu.VMEM)] * (len(args) - smem)
    single = not isinstance(shapes, list)
    outs = [shapes] if single else shapes
    result = pl.pallas_call(
        kernel,
        out_shape=[jax.ShapeDtypeStruct(*s) for s in outs],
        in_specs=specs,
        out_specs=[pl.BlockSpec(memory_space=pltpu.VMEM)] * len(outs),
        scratch_shapes=list(scratch),
        compiler_params=pltpu.CompilerParams(vmem_limit_bytes=32 * 1024 * 1024),
    )(*args)
    return result[0] if single else result


def spread(value, axes):
    return lax.all_to_all(value, axes, split_axis=0, concat_axis=0, tiled=True)


def local(snapshots, mass_blocks, block_cols, coefficients, lumped):
    nodes = snapshots.shape[0]
    total_nodes = nodes * NX * NZ * NC
    own = jnp.transpose(snapshots, (1, 0, 2))
    width = REACH * BLOCK
    count = NX * NZ * NC
    forward = [(i, i + 1) for i in range(count - 1)]
    backward = [(i + 1, i) for i in range(count - 1)]
    low = lax.ppermute(own[:, nodes - width :, :], SPACE, forward)
    high = lax.ppermute(own[:, :width, :], SPACE, backward)

    weights = jnp.broadcast_to(coefficients.T[None], (NY, MODES, TILE))
    slots = own.reshape(3, NY, BLOCK, TILE).transpose(1, 0, 2, 3).reshape(NY, ROWS, TILE)
    snaps = spread(jnp.concatenate([slots, weights], axis=1), "y")

    mass = mass_blocks.reshape(NY, BPR, BLOCK, BLOCK).transpose(0, 2, 1, 3).reshape(NY, BLOCK, BPR * BLOCK)
    image = call(
        image_kernel,
        ((NY, ROWS, TILE), BF16),
        block_cols,
        mass,
        own,
        low,
        high,
        scratch=[pltpu.VMEM((NY + 2 * REACH, BLOCK, 3 * TILE), BF16)],
        smem=1,
    )
    image = spread(image, "y")

    swap = [(0, 1), (1, 0)]
    core = lax.axis_index("core")
    half = NY // NC
    theirs = lax.dynamic_slice(snaps, ((1 - core) * half, 0, 0), (half, ROWS, TILE))
    other_snaps = lax.ppermute(theirs, "core", swap)
    weight = lax.dynamic_slice(lumped, (lax.axis_index("y") * BLOCK,), (BLOCK,)).reshape(1, BLOCK)
    raw, norm = call(raw_kernel, [((96, TILE), F32), ((NROW, TILE), BF16)], snaps, weight)
    raw = spread(jnp.broadcast_to(raw[None], (NY, 96, TILE)), "y")

    other_image = lax.ppermute(image, "core", swap)
    parts = call(
        gram_kernel, ((NX, 1024 + NROW, TILE), BF16), snaps, other_snaps, image, other_image, norm
    )
    parts = spread(parts, "x")
    parts = call(sum_x_kernel, ((NZ, 128 + NROW, TILE), BF16), parts)
    parts = spread(parts, "z")
    parts = call(sum_z_kernel, ((NC * NY, 24, TILE), F32), parts)
    parts = spread(parts, ("core", "y"))
    gram, modes = call(
        lambda *refs: final_kernel(total_nodes, *refs),
        [((16, TILE), F32), ((3, MODES, nodes), BF16)],
        parts,
        raw,
    )
    return gram.T, jnp.transpose(modes, (2, 0, 1))


def solution(mesh):
    fine = Mesh(mesh.devices.reshape(NX, NZ, NC, NY), ("x", "z", "core", "y"))
    return jax.shard_map(
        local,
        mesh=fine,
        in_specs=(
            P(SPACE, None, "y"),
            P(SPACE, None, None),
            P(SPACE, None),
            P("y", None),
            P(SPACE),
        ),
        out_specs=(P("y", SPACE), P(SPACE, None, None)),
        check_vma=False,
    )
```

```python
import jax
import jax.numpy as jnp
from jax import lax
from jax.experimental import pallas as pl
from jax.experimental.pallas import tpu as pltpu
from jax.sharding import Mesh, PartitionSpec as P

BLOCK = 64
BPR = 7
REACH = 3
NX, NZ, NC, NY = 4, 8, 2, 8
NSPACE = NX * NZ * NC
MODES = 64
TILE = 128
OWN = 16
SLOT = 24
F32 = jnp.float32
BF16 = jnp.bfloat16
SPACE = ("x", "z", "core")
ALONG = (((0,), (0,)), ((), ()))


def dual_kernel(cols, mass, own, low, mid, high, acc):
    blocks = own.shape[1] // BLOCK
    index = (lax.axis_index("x") * NZ + lax.axis_index("z")) * NC + lax.axis_index("core")
    first = index * blocks - REACH
    acc[...] = jnp.zeros_like(acc)
    for b in range(blocks):
        rows = slice(b * BLOCK, (b + 1) * BLOCK)
        right = jnp.concatenate([own[c, rows, :] for c in range(3)], axis=1)
        terms = lax.dot_general(mass[b], right, ALONG, preferred_element_type=F32)
        for j in range(BPR):
            place = cols[b, j] - first
            acc[place] += terms[j * BLOCK : (j + 1) * BLOCK]
    low[...] = acc[:REACH]
    mid[...] = acc[REACH : REACH + blocks]
    high[...] = acc[REACH + blocks :]


def join_kernel(mid, from_prev, from_next, out):
    blocks = mid.shape[0]
    for b in range(blocks):
        value = mid[b]
        if b < REACH:
            value = value + from_prev[b]
        if b >= blocks - REACH:
            value = value + from_next[b - blocks + REACH]
        high = value.astype(BF16)
        rest = (value - high.astype(F32)).astype(BF16)
        for c in range(3):
            rows = slice((c * blocks + b) * BLOCK, (c * blocks + b + 1) * BLOCK)
            lanes = slice(c * TILE, (c + 1) * TILE)
            out[rows, :TILE] = high[:, lanes]
            out[rows, TILE:] = rest[:, lanes]


def tile_products(tile, dual):
    rows = dual.shape[0]
    snaps = tile[:rows, :]
    both = lax.dot_general(snaps, dual, ALONG, preferred_element_type=F32)
    raw = lax.dot_general(
        tile[rows:, :], snaps, (((1,), (1,)), ((), ())), preferred_element_type=F32
    )
    return (both[:, :TILE] + both[:, TILE:]).astype(BF16), raw


def early_kernel(count, dual, lumped, *refs):
    tiles, gram, raw_out, lumped_out = refs[:count], refs[count], refs[count + 1], refs[count + 2]
    lumped_out[...] = lumped[...]
    for i in range(count):
        part, raw = tile_products(tiles[i][...], dual[...])
        gram[i] = part
        if i:
            raw_out[...] += raw
        else:
            raw_out[...] = raw


def late_kernel(near, dual, early, raw_in, lumped, forward, backward, half_a, half_b, slots, raw_out):
    me = lax.axis_index("y")
    nodes = raw_out.shape[2]
    far = jnp.concatenate([half_a[...], half_b[...]], axis=0)
    raw = raw_in[...]
    products = []
    for tile in (forward[...], backward[...], far):
        part, term = tile_products(tile, dual[...])
        products.append(part)
        raw = raw + term
    column = jnp.zeros((MODES, 1), F32)
    for c in range(3):
        part = raw[:, c * nodes : (c + 1) * nodes]
        raw_out[c] = part
        column = column + jnp.sum(lumped[...] * part * part, axis=1, keepdims=True)
    k = lax.broadcasted_iota(jnp.int32, (MODES, TILE), 0)
    lane = lax.broadcasted_iota(jnp.int32, (MODES, TILE), 1)
    row = jnp.sum(jnp.where(lane % MODES == k, column, 0.0), axis=0, keepdims=True)
    high = row.astype(BF16)
    rest = (row - high.astype(F32)).astype(BF16)
    lane = lax.broadcasted_iota(jnp.int32, (1, TILE), 1)
    both = jnp.where(lane < MODES, high.astype(F32), rest.astype(F32))
    norm = jnp.broadcast_to(both, (SLOT - OWN, TILE)).astype(BF16)
    steps = near + [3, NY - 3, 4]
    for i, step in enumerate(steps):
        source = lax.rem(me + step, NY)
        for o in range(TILE // OWN):
            rows = slice(o * OWN, (o + 1) * OWN)
            part = early[i, rows, :] if i < len(near) else products[i - len(near)][rows]
            slots[source * (TILE // OWN) + o] = jnp.concatenate([part, norm], axis=0)


def final_kernel(count, parts, raw, gram, modes):
    total = parts[0].astype(F32)
    for i in range(1, NSPACE):
        total = total + parts[i].astype(F32)
    gram[...] = total[:OWN] * count ** (-0.5)
    row = total[OWN : OWN + 1]
    row = row + pltpu.roll(row, MODES, 1)
    row = lax.rsqrt(row / count + 1e-06)
    k = lax.broadcasted_iota(jnp.int32, (MODES, TILE), 0)
    lane = lax.broadcasted_iota(jnp.int32, (MODES, TILE), 1)
    column = jnp.sum(jnp.where(lane == k, row, 0.0), axis=1, keepdims=True)
    for c in range(3):
        modes[c] = (raw[c] * column).astype(BF16)


def call(kernel, shapes, *args, scratch=(), smem=0):
    specs = [pl.BlockSpec(memory_space=pltpu.SMEM)] * smem
    specs += [pl.BlockSpec(memory_space=pltpu.VMEM)] * (len(args) - smem)
    single = not isinstance(shapes, list)
    outs = [shapes] if single else shapes
    result = pl.pallas_call(
        kernel,
        out_shape=[jax.ShapeDtypeStruct(*s) for s in outs],
        in_specs=specs,
        out_specs=[pl.BlockSpec(memory_space=pltpu.VMEM)] * len(outs),
        scratch_shapes=list(scratch),
        compiler_params=pltpu.CompilerParams(vmem_limit_bytes=32 * 1024 * 1024),
    )(*args)
    return result[0] if single else result


def shift(value, step):
    return lax.ppermute(value, "y", [(i, (i + step) % NY) for i in range(NY)])


def local(snapshots, mass_blocks, block_cols, coefficients, lumped):
    nodes = snapshots.shape[0]
    blocks = nodes // BLOCK
    own = jnp.transpose(snapshots, (1, 0, 2))
    tile = jnp.concatenate([own.reshape(3 * nodes, TILE), coefficients.T], axis=0)
    rows = tile.shape[0]

    mass = mass_blocks.reshape(blocks, BPR, BLOCK, BLOCK).transpose(0, 2, 1, 3)
    mass = mass.reshape(blocks, BLOCK, BPR * BLOCK)
    up, down = [tile], [tile]
    up.append(shift(tile, -1))
    down.append(shift(tile, 1))
    edge = ((REACH, BLOCK, 3 * TILE), F32)
    low, mid, high = call(
        dual_kernel,
        [edge, ((blocks, BLOCK, 3 * TILE), F32), edge],
        block_cols,
        mass,
        own,
        scratch=[pltpu.VMEM((blocks + 2 * REACH, BLOCK, 3 * TILE), F32)],
        smem=1,
    )
    second, third, low, high = lax.optimization_barrier((up[1], down[1], low, high))
    up.append(shift(second, -1))
    down.append(shift(third, 1))
    from_prev = lax.ppermute(high, SPACE, [(i, i + 1) for i in range(NSPACE - 1)])
    from_next = lax.ppermute(low, SPACE, [(i + 1, i) for i in range(NSPACE - 1)])
    dual = call(join_kernel, ((3 * nodes, 2 * TILE), BF16), mid, from_prev, from_next)

    up.append(shift(up[2], -1))
    down.append(shift(down[2], 1))
    half_a = shift(up[3][: rows // 2], -1)
    half_b = shift(down[3][rows // 2 :], 1)

    near = [0, 1, NY - 1, 2, NY - 2]
    early, raw, weight = call(
        lambda *refs: early_kernel(len(near), *refs),
        [((len(near), TILE, TILE), BF16), ((MODES, 3 * nodes), F32), ((1, nodes), F32)],
        dual,
        lumped.reshape(1, nodes),
        tile,
        up[1],
        down[1],
        up[2],
        down[2],
    )
    slots, raw = call(
        lambda *refs: late_kernel(near, *refs),
        [((NSPACE, SLOT, TILE), BF16), ((3, MODES, nodes), F32)],
        dual,
        early,
        raw,
        weight,
        up[3],
        down[3],
        half_a,
        half_b,
    )
    parts = lax.all_to_all(slots, SPACE, split_axis=0, concat_axis=0, tiled=True)
    gram, modes = call(
        lambda *refs: final_kernel(3.0 * nodes * NSPACE, *refs),
        [((OWN, TILE), F32), ((3, MODES, nodes), BF16)],
        parts,
        raw,
    )
    return gram.T, jnp.transpose(modes, (2, 0, 1))


def solution(mesh):
    fine = Mesh(mesh.devices.reshape(NX, NZ, NC, NY), ("x", "z", "core", "y"))
    return jax.shard_map(
        local,
        mesh=fine,
        in_specs=(
            P(SPACE, None, "y"),
            P(SPACE, None, None),
            P(SPACE, None),
            P("y", None),
            P(SPACE),
        ),
        out_specs=(P("y", SPACE), P(SPACE, None, None)),
        check_vma=False,
    )
```

```python
import jax
import jax.numpy as jnp
from jax import lax
from jax.experimental import pallas as pl
from jax.experimental.pallas import tpu as pltpu
from jax.sharding import Mesh, PartitionSpec as P

BLOCK = 64
BPR = 7
REACH = 3
NX, NZ, NC, NY = 4, 8, 2, 8
NSPACE = NX * NZ * NC
MODES = 64
TILE = 128
OWN = 16
SLOT = 24
F32 = jnp.float32
BF16 = jnp.bfloat16
SPACE = ("x", "z", "core")
ALONG = (((0,), (0,)), ((), ()))


def dual_kernel(cols, mass, own, low, mid, high, acc):
    blocks = own.shape[1] // BLOCK
    index = (lax.axis_index("x") * NZ + lax.axis_index("z")) * NC + lax.axis_index("core")
    first = index * blocks - REACH
    acc[...] = jnp.zeros_like(acc)
    for b in range(blocks):
        rows = slice(b * BLOCK, (b + 1) * BLOCK)
        right = jnp.concatenate([own[c, rows, :] for c in range(3)], axis=1)
        left = jnp.concatenate([mass[j, b] for j in range(BPR)], axis=1)
        terms = lax.dot_general(left, right, ALONG, preferred_element_type=F32)
        for j in range(BPR):
            place = cols[b, j] - first
            acc[place] += terms[j * BLOCK : (j + 1) * BLOCK]
    low[...] = acc[:REACH]
    mid[...] = acc[REACH : REACH + blocks]
    high[...] = acc[REACH + blocks :]


def join_kernel(mid, from_prev, from_next, out):
    blocks = mid.shape[0]
    for b in range(blocks):
        value = mid[b]
        if b < REACH:
            value = value + from_prev[b]
        if b >= blocks - REACH:
            value = value + from_next[b - blocks + REACH]
        high = value.astype(BF16)
        rest = (value - high.astype(F32)).astype(BF16)
        for c in range(3):
            rows = slice((c * blocks + b) * BLOCK, (c * blocks + b + 1) * BLOCK)
            lanes = slice(c * TILE, (c + 1) * TILE)
            out[rows, :TILE] = high[:, lanes]
            out[rows, TILE:] = rest[:, lanes]


def tile_products(tile, dual):
    rows = dual.shape[0]
    snaps = tile[:rows, :]
    both = lax.dot_general(snaps, dual, ALONG, preferred_element_type=F32)
    raw = lax.dot_general(
        tile[rows:, :], snaps, (((1,), (1,)), ((), ())), preferred_element_type=F32
    )
    return both[:, :TILE] + both[:, TILE:], raw


def early_kernel(count, dual, lumped, *refs):
    tiles, gram, raw_out, lumped_out = refs[:count], refs[count], refs[count + 1], refs[count + 2]
    lumped_out[...] = lumped[...]
    for i in range(count):
        part, raw = tile_products(tiles[i][...], dual[...])
        gram[i] = part
        if i:
            raw_out[...] += raw
        else:
            raw_out[...] = raw


def late_kernel(near, dual, early, raw_in, lumped, forward, backward, half_a, half_b, mine, other, raw_out):
    me = lax.axis_index("y")
    nodes = raw_out.shape[2]
    far = jnp.concatenate([half_a[...], half_b[...]], axis=0)
    raw = raw_in[...]
    products = []
    for tile in (forward[...], backward[...], far):
        part, term = tile_products(tile, dual[...])
        products.append(part)
        raw = raw + term
    column = jnp.zeros((MODES, 1), F32)
    for c in range(3):
        part = raw[:, c * nodes : (c + 1) * nodes]
        raw_out[c] = part
        column = column + jnp.sum(lumped[...] * part * part, axis=1, keepdims=True)
    k = lax.broadcasted_iota(jnp.int32, (MODES, TILE), 0)
    lane = lax.broadcasted_iota(jnp.int32, (MODES, TILE), 1)
    row = jnp.sum(jnp.where(lane % MODES == k, column, 0.0), axis=0, keepdims=True)
    norm = jnp.broadcast_to(row, (SLOT - OWN, TILE))
    steps = near + [3, NY - 3, 4]
    first = lax.axis_index("core") == 0
    for i, step in enumerate(steps):
        source = lax.rem(me + step, NY)
        part = early[i] if i < len(near) else products[i - len(near)]
        for o in range(TILE // OWN // NC):
            one = part[2 * o * OWN : (2 * o + 1) * OWN]
            two = part[(2 * o + 1) * OWN : (2 * o + 2) * OWN]
            place = source * (TILE // OWN // NC) + o
            mine[place, :OWN, :] = jnp.where(first, one, two)
            other[place, :OWN, :] = jnp.where(first, two, one)
    for i in range(NSPACE // NC):
        mine[i, OWN:, :] = norm
        other[i, OWN:, :] = norm


def pair_kernel(mine, other, out):
    lane = lax.broadcasted_iota(jnp.int32, (SLOT - OWN, TILE), 1)
    row = mine[0, OWN:, :] + other[0, OWN:, :]
    high = row.astype(BF16)
    rest = (row - high.astype(F32)).astype(BF16)
    norm = jnp.where(lane < MODES, high.astype(F32), rest.astype(F32))
    for i in range(NSPACE // NC):
        total = mine[i, :OWN, :] + other[i, :OWN, :]
        out[i] = jnp.concatenate([total, norm], axis=0).astype(BF16)


def final_kernel(count, parts, raw, gram, modes):
    total = parts[0].astype(F32)
    for i in range(1, NSPACE // NC):
        total = total + parts[i].astype(F32)
    gram[...] = total[:OWN] * count ** (-0.5)
    row = total[OWN : OWN + 1]
    row = row + pltpu.roll(row, MODES, 1)
    row = lax.rsqrt(row / count + 1e-06)
    k = lax.broadcasted_iota(jnp.int32, (MODES, TILE), 0)
    lane = lax.broadcasted_iota(jnp.int32, (MODES, TILE), 1)
    column = jnp.sum(jnp.where(lane == k, row, 0.0), axis=1, keepdims=True)
    for c in range(3):
        modes[c] = (raw[c] * column).astype(BF16)


def call(kernel, shapes, *args, scratch=(), smem=0):
    specs = [pl.BlockSpec(memory_space=pltpu.SMEM)] * smem
    specs += [pl.BlockSpec(memory_space=pltpu.VMEM)] * (len(args) - smem)
    single = not isinstance(shapes, list)
    outs = [shapes] if single else shapes
    result = pl.pallas_call(
        kernel,
        out_shape=[jax.ShapeDtypeStruct(*s) for s in outs],
        in_specs=specs,
        out_specs=[pl.BlockSpec(memory_space=pltpu.VMEM)] * len(outs),
        scratch_shapes=list(scratch),
        compiler_params=pltpu.CompilerParams(vmem_limit_bytes=32 * 1024 * 1024),
    )(*args)
    return result[0] if single else result


def shift(value, step):
    return lax.ppermute(value, "y", [(i, (i + step) % NY) for i in range(NY)])


def local(snapshots, mass_blocks, block_cols, coefficients, lumped):
    nodes = snapshots.shape[0]
    blocks = nodes // BLOCK
    own = jnp.transpose(snapshots, (1, 0, 2))
    tile = jnp.concatenate([own.reshape(3 * nodes, TILE), coefficients.T], axis=0)
    cut = tile.shape[0] // 2

    mass = mass_blocks.reshape(blocks, BPR, BLOCK, BLOCK).transpose(1, 0, 2, 3)
    up, down = [tile], [tile]
    up.append(shift(tile, -1))
    down.append(shift(tile, 1))
    edge = ((REACH, BLOCK, 3 * TILE), F32)
    low, mid, high = call(
        dual_kernel,
        [edge, ((blocks, BLOCK, 3 * TILE), F32), edge],
        block_cols,
        mass,
        own,
        scratch=[pltpu.VMEM((blocks + 2 * REACH, BLOCK, 3 * TILE), F32)],
        smem=1,
    )
    first, low, high = lax.optimization_barrier((up[1], low, high))
    up.append(shift(first, -1))
    down.append(shift(down[1], 1))
    low, high, down[1] = lax.optimization_barrier((low, high, down[1]))
    from_prev = lax.ppermute(high, SPACE, [(i, i + 1) for i in range(NSPACE - 1)])
    from_next = lax.ppermute(low, SPACE, [(i + 1, i) for i in range(NSPACE - 1)])
    up.append(shift(up[2], -1))
    down.append(shift(down[2], 1))
    dual = call(join_kernel, ((3 * nodes, 2 * TILE), BF16), mid, from_prev, from_next)

    half_a = shift(up[3][:cut], -1)
    half_b = shift(down[3][cut:], 1)

    near = [0, 1, NY - 1, 2, NY - 2]
    early, raw, weight = call(
        lambda *refs: early_kernel(len(near), *refs),
        [((len(near), TILE, TILE), F32), ((MODES, 3 * nodes), F32), ((1, nodes), F32)],
        dual,
        lumped.reshape(1, nodes),
        tile,
        up[1],
        down[1],
        up[2],
        down[2],
    )
    slot = ((NSPACE // NC, SLOT, TILE), F32)
    mine, other, raw = call(
        lambda *refs: late_kernel(near, *refs),
        [slot, slot, ((3, MODES, nodes), F32)],
        dual,
        early,
        raw,
        weight,
        up[3],
        down[3],
        half_a,
        half_b,
    )
    other = lax.ppermute(other, "core", [(0, 1), (1, 0)])
    slots = call(pair_kernel, ((NSPACE // NC, SLOT, TILE), BF16), mine, other)
    parts = lax.all_to_all(slots, ("x", "z"), split_axis=0, concat_axis=0, tiled=True)
    gram, modes = call(
        lambda *refs: final_kernel(3.0 * nodes * NSPACE, *refs),
        [((OWN, TILE), F32), ((3, MODES, nodes), BF16)],
        parts,
        raw,
    )
    return gram.T, jnp.transpose(modes, (2, 0, 1))


def solution(mesh):
    fine = Mesh(mesh.devices.reshape(NX, NZ, NC, NY), ("x", "z", "core", "y"))
    return jax.shard_map(
        local,
        mesh=fine,
        in_specs=(
            P(SPACE, None, "y"),
            P(SPACE, None, None),
            P(SPACE, None),
            P("y", None),
            P(SPACE),
        ),
        out_specs=(P("y", SPACE), P(SPACE, None, None)),
        check_vma=False,
    )
```

```python
import jax
import jax.numpy as jnp
from jax import lax
from jax.experimental import pallas as pl
from jax.experimental.pallas import tpu as pltpu
from jax.sharding import Mesh, PartitionSpec as P

BLOCK = 64
BPR = 7
REACH = 3
NX, NZ, NC, NY = 4, 8, 2, 8
NSPACE = NX * NZ * NC
MODES = 64
TILE = 128
OWN = 16
SLOT = 24
F32 = jnp.float32
BF16 = jnp.bfloat16
SPACE = ("x", "z", "core")
ALONG = (((0,), (0,)), ((), ()))


def dual_kernel(cols, mass, own, lumped, low, mid, high, weight, acc):
    weight[...] = lumped[...]
    blocks = own.shape[1] // BLOCK
    index = (lax.axis_index("x") * NZ + lax.axis_index("z")) * NC + lax.axis_index("core")
    first = index * blocks - REACH
    acc[...] = jnp.zeros_like(acc)
    for b in range(blocks):
        rows = slice(b * BLOCK, (b + 1) * BLOCK)
        right = jnp.concatenate([own[c, rows, :] for c in range(3)], axis=1)
        left = jnp.concatenate([mass[j, b] for j in range(BPR)], axis=1)
        terms = lax.dot_general(left, right, ALONG, preferred_element_type=F32)
        for j in range(BPR):
            place = cols[b, j] - first
            acc[place] += terms[j * BLOCK : (j + 1) * BLOCK]
    low[...] = acc[:REACH]
    mid[...] = acc[REACH : REACH + blocks]
    high[...] = acc[REACH + blocks :]


def join_kernel(mid, from_prev, from_next, out):
    blocks = mid.shape[0]
    for b in range(blocks):
        value = mid[b]
        if b < REACH:
            value = value + from_prev[b]
        if b >= blocks - REACH:
            value = value + from_next[b - blocks + REACH]
        high = value.astype(BF16)
        rest = (value - high.astype(F32)).astype(BF16)
        for c in range(3):
            rows = slice((c * blocks + b) * BLOCK, (c * blocks + b + 1) * BLOCK)
            lanes = slice(c * TILE, (c + 1) * TILE)
            out[rows, :TILE] = high[:, lanes]
            out[rows, TILE:] = rest[:, lanes]


def gram_product(tile, dual):
    both = lax.dot_general(tile[: dual.shape[0], :], dual, ALONG, preferred_element_type=F32)
    return both[:, :TILE] + both[:, TILE:]


def raw_product(tile):
    rows = tile.shape[0] - MODES
    return lax.dot_general(
        tile[rows:, :], tile[:rows, :], (((1,), (1,)), ((), ())), preferred_element_type=F32
    )


def first_kernel(own, one, two, raw_out):
    raw_out[...] = raw_product(own[...]) + raw_product(one[...]) + raw_product(two[...])


def early_kernel(count, dual, raw_in, *refs):
    tiles, gram, raw_out = refs[:count], refs[count], refs[count + 1]
    raw = raw_in[...]
    for i in range(count):
        tile = tiles[i][...]
        gram[i] = gram_product(tile, dual[...])
        if i >= 3:
            raw = raw + raw_product(tile)
    raw_out[...] = raw


def late_kernel(near, dual, early, raw_in, lumped, half_a, half_b, mine, other, norm_out, raw_out):
    me = lax.axis_index("y")
    nodes = raw_out.shape[2]
    far = jnp.concatenate([half_a[...], half_b[...]], axis=0)
    product = gram_product(far, dual[...])
    raw = raw_in[...] + raw_product(far)
    column = jnp.zeros((MODES, 1), F32)
    for c in range(3):
        part = raw[:, c * nodes : (c + 1) * nodes]
        raw_out[c] = part
        column = column + jnp.sum(lumped[...] * part * part, axis=1, keepdims=True)
    k = lax.broadcasted_iota(jnp.int32, (MODES, TILE), 0)
    lane = lax.broadcasted_iota(jnp.int32, (MODES, TILE), 1)
    row = jnp.sum(jnp.where(lane % MODES == k, column, 0.0), axis=0, keepdims=True)
    norm_out[...] = jnp.broadcast_to(row, (SLOT - OWN, TILE))
    other[NSPACE // NC] = jnp.broadcast_to(row, (OWN, TILE))
    steps = near + [4]
    first = lax.axis_index("core") == 0
    for i, step in enumerate(steps):
        source = lax.rem(me + step, NY)
        part = early[i] if i < len(near) else product
        for o in range(TILE // OWN // NC):
            one = part[2 * o * OWN : (2 * o + 1) * OWN]
            two = part[(2 * o + 1) * OWN : (2 * o + 2) * OWN]
            place = source * (TILE // OWN // NC) + o
            mine[place] = jnp.where(first, one, two)
            other[place] = jnp.where(first, two, one)


def pair_kernel(mine, other, norm_in, out):
    lane = lax.broadcasted_iota(jnp.int32, (SLOT - OWN, TILE), 1)
    row = norm_in[...] + other[NSPACE // NC, : SLOT - OWN, :]
    high = row.astype(BF16)
    rest = (row - high.astype(F32)).astype(BF16)
    norm = jnp.where(lane < MODES, high.astype(F32), rest.astype(F32))
    for i in range(NSPACE // NC):
        total = mine[i] + other[i]
        out[i] = jnp.concatenate([total, norm], axis=0).astype(BF16)


def final_kernel(count, parts, raw, gram, modes):
    total = parts[0].astype(F32)
    for i in range(1, NSPACE // NC):
        total = total + parts[i].astype(F32)
    gram[...] = total[:OWN] * count ** (-0.5)
    row = total[OWN : OWN + 1]
    row = row + pltpu.roll(row, MODES, 1)
    row = lax.rsqrt(row / count + 1e-06)
    k = lax.broadcasted_iota(jnp.int32, (MODES, TILE), 0)
    lane = lax.broadcasted_iota(jnp.int32, (MODES, TILE), 1)
    column = jnp.sum(jnp.where(lane == k, row, 0.0), axis=1, keepdims=True)
    for c in range(3):
        modes[c] = (raw[c] * column).astype(BF16)


def call(kernel, shapes, *args, scratch=(), smem=0):
    specs = [pl.BlockSpec(memory_space=pltpu.SMEM)] * smem
    specs += [pl.BlockSpec(memory_space=pltpu.VMEM)] * (len(args) - smem)
    single = not isinstance(shapes, list)
    outs = [shapes] if single else shapes
    result = pl.pallas_call(
        kernel,
        out_shape=[jax.ShapeDtypeStruct(*s) for s in outs],
        in_specs=specs,
        out_specs=[pl.BlockSpec(memory_space=pltpu.VMEM)] * len(outs),
        scratch_shapes=list(scratch),
        compiler_params=pltpu.CompilerParams(vmem_limit_bytes=32 * 1024 * 1024),
    )(*args)
    return result[0] if single else result


def shift(value, step):
    return lax.ppermute(value, "y", [(i, (i + step) % NY) for i in range(NY)])


def local(snapshots, mass_blocks, block_cols, coefficients, lumped):
    nodes = snapshots.shape[0]
    blocks = nodes // BLOCK
    own = jnp.transpose(snapshots, (1, 0, 2))
    tile = jnp.concatenate([own.reshape(3 * nodes, TILE), coefficients.T], axis=0)
    cut = tile.shape[0] // 2

    mass = mass_blocks.reshape(blocks, BPR, BLOCK, BLOCK).transpose(1, 0, 2, 3)
    up, down = [tile], [tile]
    up.append(shift(tile, -1))
    down.append(shift(tile, 1))
    edge = ((REACH, BLOCK, 3 * TILE), F32)
    low, mid, high, weight = call(
        dual_kernel,
        [edge, ((blocks, BLOCK, 3 * TILE), F32), edge, ((1, nodes), F32)],
        block_cols,
        mass,
        own,
        lumped.reshape(1, nodes),
        scratch=[pltpu.VMEM((blocks + 2 * REACH, BLOCK, 3 * TILE), F32)],
        smem=1,
    )
    first, low, high = lax.optimization_barrier((up[1], low, high))
    up.append(shift(first, -1))
    down.append(shift(down[1], 1))
    low, high, down[1] = lax.optimization_barrier((low, high, down[1]))
    from_prev = lax.ppermute(high, SPACE, [(i, i + 1) for i in range(NSPACE - 1)])
    from_next = lax.ppermute(low, SPACE, [(i + 1, i) for i in range(NSPACE - 1)])
    raw = call(first_kernel, ((MODES, 3 * nodes), F32), tile, up[1], down[1])
    second, raw = lax.optimization_barrier((up[2], raw))
    up.append(shift(second, -1))
    down.append(shift(down[2], 1))
    dual = call(join_kernel, ((3 * nodes, 2 * TILE), BF16), mid, from_prev, from_next)

    half_a = shift(up[3][:cut], -1)
    half_b = shift(down[3][cut:], 1)

    near = [0, 1, NY - 1, 2, NY - 2, 3, NY - 3]
    early, raw = call(
        lambda *refs: early_kernel(len(near), *refs),
        [((len(near), TILE, TILE), F32), ((MODES, 3 * nodes), F32)],
        dual,
        raw,
        tile,
        up[1],
        down[1],
        up[2],
        down[2],
        up[3],
        down[3],
    )
    own_slots = ((NSPACE // NC, OWN, TILE), F32)
    far_slots = ((NSPACE // NC + 1, OWN, TILE), F32)
    mine, other, norm, raw = call(
        lambda *refs: late_kernel(near, *refs),
        [own_slots, far_slots, ((SLOT - OWN, TILE), F32), ((3, MODES, nodes), F32)],
        dual,
        early,
        raw,
        weight,
        half_a,
        half_b,
    )
    other = lax.ppermute(other, "core", [(0, 1), (1, 0)])
    slots = call(pair_kernel, ((NSPACE // NC, SLOT, TILE), BF16), mine, other, norm)
    parts = lax.all_to_all(slots, ("x", "z"), split_axis=0, concat_axis=0, tiled=True)
    gram, modes = call(
        lambda *refs: final_kernel(3.0 * nodes * NSPACE, *refs),
        [((OWN, TILE), F32), ((3, MODES, nodes), BF16)],
        parts,
        raw,
    )
    return gram.T, jnp.transpose(modes, (2, 0, 1))


def solution(mesh):
    fine = Mesh(mesh.devices.reshape(NX, NZ, NC, NY), ("x", "z", "core", "y"))
    return jax.shard_map(
        local,
        mesh=fine,
        in_specs=(
            P(SPACE, None, "y"),
            P(SPACE, None, None),
            P(SPACE, None),
            P("y", None),
            P(SPACE),
        ),
        out_specs=(P("y", SPACE), P(SPACE, None, None)),
        check_vma=False,
    )
```

```python
import jax
import jax.numpy as jnp
from jax import lax
from jax.experimental import pallas as pl
from jax.experimental.pallas import tpu as pltpu
from jax.sharding import Mesh, PartitionSpec as P

BLOCK = 64
BPR = 7
REACH = 3
NX, NZ, NC, NY = 4, 8, 2, 8
NSPACE = NX * NZ * NC
MODES = 64
TILE = 128
OWN = 16
SLOT = 24
F32 = jnp.float32
BF16 = jnp.bfloat16
SPACE = ("x", "z", "core")
ALONG = (((0,), (0,)), ((), ()))


def dual_kernel(cols, mass, own, lumped, low, mid, high, weight, acc):
    weight[...] = lumped[...]
    blocks = own.shape[1] // BLOCK
    index = (lax.axis_index("x") * NZ + lax.axis_index("z")) * NC + lax.axis_index("core")
    first = index * blocks - REACH
    acc[...] = jnp.zeros_like(acc)
    for b in range(blocks):
        rows = slice(b * BLOCK, (b + 1) * BLOCK)
        right = jnp.concatenate([own[c, rows, :] for c in range(3)], axis=1)
        left = jnp.concatenate([mass[j, b] for j in range(BPR)], axis=1)
        terms = lax.dot_general(left, right, ALONG, preferred_element_type=F32)
        for j in range(BPR):
            place = cols[b, j] - first
            acc[place] += terms[j * BLOCK : (j + 1) * BLOCK]
    low[...] = acc[:REACH]
    mid[...] = acc[REACH : REACH + blocks]
    high[...] = acc[REACH + blocks :]


def join_kernel(mid, from_next, from_prev, out):
    blocks = mid.shape[0]
    for b in range(blocks):
        value = mid[b]
        if b < REACH:
            value = value + from_prev[b]
        if b >= blocks - REACH:
            value = value + from_next[b - blocks + REACH]
        high = value.astype(BF16)
        rest = (value - high.astype(F32)).astype(BF16)
        for c in range(3):
            rows = slice((c * blocks + b) * BLOCK, (c * blocks + b + 1) * BLOCK)
            lanes = slice(c * TILE, (c + 1) * TILE)
            out[rows, :TILE] = high[:, lanes]
            out[rows, TILE:] = rest[:, lanes]


def gram_product(tile, dual):
    both = lax.dot_general(tile[: dual.shape[0], :], dual, ALONG, preferred_element_type=F32)
    return both[:, :TILE] + both[:, TILE:]


def raw_product(tile):
    rows = tile.shape[0] - MODES
    return lax.dot_general(
        tile[rows:, :], tile[:rows, :], (((1,), (1,)), ((), ())), preferred_element_type=F32
    )


def first_kernel(own, one, two, raw_out):
    raw_out[...] = raw_product(own[...]) + raw_product(one[...]) + raw_product(two[...])


def early_kernel(count, dual, raw_in, *refs):
    tiles, gram, raw_out = refs[:count], refs[count], refs[count + 1]
    raw = raw_in[...]
    for i in range(count):
        tile = tiles[i][...]
        gram[i] = gram_product(tile, dual[...])
        if i >= 3:
            raw = raw + raw_product(tile)
    raw_out[...] = raw


def late_kernel(near, dual, early, raw_in, lumped, half_a, half_b, mine, other, norm_out, raw_out):
    me = lax.axis_index("y")
    nodes = raw_out.shape[2]
    far = jnp.concatenate([half_a[...], half_b[...]], axis=0)
    product = gram_product(far, dual[...])
    raw = raw_in[...] + raw_product(far)
    column = jnp.zeros((MODES, 1), F32)
    for c in range(3):
        part = raw[:, c * nodes : (c + 1) * nodes]
        raw_out[c] = part
        column = column + jnp.sum(lumped[...] * part * part, axis=1, keepdims=True)
    k = lax.broadcasted_iota(jnp.int32, (MODES, TILE), 0)
    lane = lax.broadcasted_iota(jnp.int32, (MODES, TILE), 1)
    row = jnp.sum(jnp.where(lane % MODES == k, column, 0.0), axis=0, keepdims=True)
    norm_out[...] = jnp.broadcast_to(row, (SLOT - OWN, TILE))
    other[NSPACE // NC] = jnp.broadcast_to(row, (OWN, TILE))
    steps = near + [4]
    first = lax.axis_index("core") == 0
    for i, step in enumerate(steps):
        source = lax.rem(me + step, NY)
        part = early[i] if i < len(near) else product
        for o in range(TILE // OWN // NC):
            one = part[2 * o * OWN : (2 * o + 1) * OWN]
            two = part[(2 * o + 1) * OWN : (2 * o + 2) * OWN]
            place = source * (TILE // OWN // NC) + o
            mine[place] = jnp.where(first, one, two)
            other[place] = jnp.where(first, two, one)


def pair_kernel(mine, other, norm_in, out):
    lane = lax.broadcasted_iota(jnp.int32, (SLOT - OWN, TILE), 1)
    row = norm_in[...] + other[NSPACE // NC, : SLOT - OWN, :]
    high = row.astype(BF16)
    rest = (row - high.astype(F32)).astype(BF16)
    norm = jnp.where(lane < MODES, high.astype(F32), rest.astype(F32))
    for i in range(NSPACE // NC):
        total = mine[i] + other[i]
        out[i] = jnp.concatenate([total, norm], axis=0).astype(BF16)


def final_kernel(count, parts, raw, gram, modes):
    total = parts[0].astype(F32)
    for i in range(1, NSPACE // NC):
        total = total + parts[i].astype(F32)
    gram[...] = total[:OWN] * count ** (-0.5)
    row = total[OWN : OWN + 1]
    row = row + pltpu.roll(row, MODES, 1)
    row = lax.rsqrt(row / count + 1e-06)
    k = lax.broadcasted_iota(jnp.int32, (MODES, TILE), 0)
    lane = lax.broadcasted_iota(jnp.int32, (MODES, TILE), 1)
    column = jnp.sum(jnp.where(lane == k, row, 0.0), axis=1, keepdims=True)
    for c in range(3):
        modes[c] = (raw[c] * column).astype(BF16)


def call(kernel, shapes, *args, scratch=(), smem=0):
    specs = [pl.BlockSpec(memory_space=pltpu.SMEM)] * smem
    specs += [pl.BlockSpec(memory_space=pltpu.VMEM)] * (len(args) - smem)
    single = not isinstance(shapes, list)
    outs = [shapes] if single else shapes
    result = pl.pallas_call(
        kernel,
        out_shape=[jax.ShapeDtypeStruct(*s) for s in outs],
        in_specs=specs,
        out_specs=[pl.BlockSpec(memory_space=pltpu.VMEM)] * len(outs),
        scratch_shapes=list(scratch),
        compiler_params=pltpu.CompilerParams(vmem_limit_bytes=32 * 1024 * 1024),
    )(*args)
    return result[0] if single else result


def shift(value, step):
    return lax.ppermute(value, "y", [(i, (i + step) % NY) for i in range(NY)])


def local(snapshots, mass_blocks, block_cols, coefficients, lumped):
    nodes = snapshots.shape[0]
    blocks = nodes // BLOCK
    own = jnp.transpose(snapshots, (1, 0, 2))
    tile = jnp.concatenate([own.reshape(3 * nodes, TILE), coefficients.T], axis=0)
    cut = tile.shape[0] // 2

    mass = mass_blocks.reshape(blocks, BPR, BLOCK, BLOCK).transpose(1, 0, 2, 3)
    up, down = [tile], [tile]
    up.append(shift(tile, -1))
    down.append(shift(tile, 1))
    edge = ((REACH, BLOCK, 3 * TILE), F32)
    low, mid, high, weight = call(
        dual_kernel,
        [edge, ((blocks, BLOCK, 3 * TILE), F32), edge, ((1, nodes), F32)],
        block_cols,
        mass,
        own,
        lumped.reshape(1, nodes),
        scratch=[pltpu.VMEM((blocks + 2 * REACH, BLOCK, 3 * TILE), F32)],
        smem=1,
    )
    first, low, high = lax.optimization_barrier((up[1], low, high))
    up.append(shift(first, -1))
    down.append(shift(down[1], 1))
    low, high, down[1] = lax.optimization_barrier((low, high, down[1]))
    from_next = lax.ppermute(low, SPACE, [(i + 1, i) for i in range(NSPACE - 1)])
    from_prev = lax.ppermute(high, SPACE, [(i, i + 1) for i in range(NSPACE - 1)])
    raw = call(first_kernel, ((MODES, 3 * nodes), F32), tile, up[1], down[1])
    second, raw = lax.optimization_barrier((up[2], raw))
    up.append(shift(second, -1))
    down.append(shift(down[2], 1))
    dual = call(join_kernel, ((3 * nodes, 2 * TILE), BF16), mid, from_next, from_prev)

    half_a = shift(up[3][:cut], -1)
    half_b = shift(down[3][cut:], 1)

    near = [0, 1, NY - 1, 2, NY - 2, 3, NY - 3]
    early, raw = call(
        lambda *refs: early_kernel(len(near), *refs),
        [((len(near), TILE, TILE), F32), ((MODES, 3 * nodes), F32)],
        dual,
        raw,
        tile,
        up[1],
        down[1],
        up[2],
        down[2],
        up[3],
        down[3],
    )
    own_slots = ((NSPACE // NC, OWN, TILE), F32)
    far_slots = ((NSPACE // NC + 1, OWN, TILE), F32)
    mine, other, norm, raw = call(
        lambda *refs: late_kernel(near, *refs),
        [own_slots, far_slots, ((SLOT - OWN, TILE), F32), ((3, MODES, nodes), F32)],
        dual,
        early,
        raw,
        weight,
        half_a,
        half_b,
    )
    other = lax.ppermute(other, "core", [(0, 1), (1, 0)])
    slots = call(pair_kernel, ((NSPACE // NC, SLOT, TILE), BF16), mine, other, norm)
    parts = lax.all_to_all(slots, ("x", "z"), split_axis=0, concat_axis=0, tiled=True)
    gram, modes = call(
        lambda *refs: final_kernel(3.0 * nodes * NSPACE, *refs),
        [((OWN, TILE), F32), ((3, MODES, nodes), BF16)],
        parts,
        raw,
    )
    return gram.T, jnp.transpose(modes, (2, 0, 1))


def solution(mesh):
    fine = Mesh(mesh.devices.reshape(NX, NZ, NC, NY), ("x", "z", "core", "y"))
    return jax.shard_map(
        local,
        mesh=fine,
        in_specs=(
            P(SPACE, None, "y"),
            P(SPACE, None, None),
            P(SPACE, None),
            P("y", None),
            P(SPACE),
        ),
        out_specs=(P("y", SPACE), P(SPACE, None, None)),
        check_vma=False,
    )
```

```python
import jax
import jax.numpy as jnp
from jax import lax
from jax.experimental import pallas as pl
from jax.experimental.pallas import tpu as pltpu
from jax.sharding import Mesh, PartitionSpec as P

BLOCK = 64
BPR = 7
REACH = 3
NX, NZ, NC, NY = 4, 8, 2, 8
NSPACE = NX * NZ * NC
MODES = 64
TILE = 128
OWN = 16
SLOT = 24
F32 = jnp.float32
BF16 = jnp.bfloat16
SPACE = ("x", "z", "core")
ALONG = (((0,), (0,)), ((), ()))


def dual_kernel(cols, mass, own, lumped, low, mid, high, weight, acc):
    weight[...] = lumped[...]
    blocks = own.shape[1] // BLOCK
    index = (lax.axis_index("x") * NZ + lax.axis_index("z")) * NC + lax.axis_index("core")
    first = index * blocks - REACH
    acc[...] = jnp.zeros_like(acc)
    for b in range(blocks):
        rows = slice(b * BLOCK, (b + 1) * BLOCK)
        right = jnp.concatenate([own[c, rows, :] for c in range(3)], axis=1)
        left = jnp.concatenate([mass[j, b] for j in range(BPR)], axis=1)
        terms = lax.dot_general(left, right, ALONG, preferred_element_type=F32)
        for j in range(BPR):
            place = cols[b, j] - first
            acc[place] += terms[j * BLOCK : (j + 1) * BLOCK]
    low[...] = acc[:REACH]
    mid[...] = acc[REACH : REACH + blocks]
    high[...] = acc[REACH + blocks :]


def join_kernel(mid, from_next, from_prev, out):
    blocks = mid.shape[0]
    for b in range(blocks):
        value = mid[b]
        if b < REACH:
            value = value + from_prev[b]
        if b >= blocks - REACH:
            value = value + from_next[b - blocks + REACH]
        high = value.astype(BF16)
        rest = (value - high.astype(F32)).astype(BF16)
        for c in range(3):
            rows = slice((c * blocks + b) * BLOCK, (c * blocks + b + 1) * BLOCK)
            lanes = slice(c * TILE, (c + 1) * TILE)
            out[rows, :TILE] = high[:, lanes]
            out[rows, TILE:] = rest[:, lanes]


def gram_product(tile, dual):
    both = lax.dot_general(tile[: dual.shape[0], :], dual, ALONG, preferred_element_type=F32)
    return both[:, :TILE] + both[:, TILE:]


def raw_product(tile):
    rows = tile.shape[0] - MODES
    return lax.dot_general(
        tile[rows:, :], tile[:rows, :], (((1,), (1,)), ((), ())), preferred_element_type=F32
    )


def first_kernel(own, one, two, raw_out):
    raw_out[...] = raw_product(own[...]) + raw_product(one[...]) + raw_product(two[...])


def early_kernel(count, dual, raw_in, *refs):
    tiles, gram, raw_out = refs[:count], refs[count], refs[count + 1]
    raw = raw_in[...]
    for i in range(count):
        tile = tiles[i][...]
        gram[i] = gram_product(tile, dual[...])
        if i >= 3:
            raw = raw + raw_product(tile)
    raw_out[...] = raw


def late_kernel(near, dual, early, raw_in, lumped, half_a, half_b, mine, other, norm_out, raw_out):
    me = lax.axis_index("y")
    nodes = raw_out.shape[2]
    far = jnp.concatenate([half_a[...], half_b[...]], axis=0)
    product = gram_product(far, dual[...])
    raw = raw_in[...] + raw_product(far)
    column = jnp.zeros((MODES, 1), F32)
    for c in range(3):
        part = raw[:, c * nodes : (c + 1) * nodes]
        raw_out[c] = part
        column = column + jnp.sum(lumped[...] * part * part, axis=1, keepdims=True)
    k = lax.broadcasted_iota(jnp.int32, (MODES, TILE), 0)
    lane = lax.broadcasted_iota(jnp.int32, (MODES, TILE), 1)
    row = jnp.sum(jnp.where(lane % MODES == k, column, 0.0), axis=0, keepdims=True)
    norm_out[...] = jnp.broadcast_to(row, (SLOT - OWN, TILE))
    other[NSPACE // NC] = jnp.broadcast_to(row, (OWN, TILE))
    turn = 1 - 2 * lax.rem(me, 2)
    steps = near + [4]
    first = lax.axis_index("core") == 0
    for i, step in enumerate(steps):
        source = lax.rem(me + step * turn + NY, NY)
        part = early[i] if i < len(near) else product
        for o in range(TILE // OWN // NC):
            one = part[2 * o * OWN : (2 * o + 1) * OWN]
            two = part[(2 * o + 1) * OWN : (2 * o + 2) * OWN]
            place = source * (TILE // OWN // NC) + o
            mine[place] = jnp.where(first, one, two)
            other[place] = jnp.where(first, two, one)


def pair_kernel(mine, other, norm_in, out):
    lane = lax.broadcasted_iota(jnp.int32, (SLOT - OWN, TILE), 1)
    row = norm_in[...] + other[NSPACE // NC, : SLOT - OWN, :]
    high = row.astype(BF16)
    rest = (row - high.astype(F32)).astype(BF16)
    norm = jnp.where(lane < MODES, high.astype(F32), rest.astype(F32))
    for i in range(NSPACE // NC):
        total = mine[i] + other[i]
        out[i] = jnp.concatenate([total, norm], axis=0).astype(BF16)


def final_kernel(count, parts, raw, gram, modes):
    total = parts[0].astype(F32)
    for i in range(1, NSPACE // NC):
        total = total + parts[i].astype(F32)
    gram[...] = total[:OWN] * count ** (-0.5)
    row = total[OWN : OWN + 1]
    row = row + pltpu.roll(row, MODES, 1)
    row = lax.rsqrt(row / count + 1e-06)
    k = lax.broadcasted_iota(jnp.int32, (MODES, TILE), 0)
    lane = lax.broadcasted_iota(jnp.int32, (MODES, TILE), 1)
    column = jnp.sum(jnp.where(lane == k, row, 0.0), axis=1, keepdims=True)
    for c in range(3):
        modes[c] = (raw[c] * column).astype(BF16)


def call(kernel, shapes, *args, scratch=(), smem=0):
    specs = [pl.BlockSpec(memory_space=pltpu.SMEM)] * smem
    specs += [pl.BlockSpec(memory_space=pltpu.VMEM)] * (len(args) - smem)
    single = not isinstance(shapes, list)
    outs = [shapes] if single else shapes
    result = pl.pallas_call(
        kernel,
        out_shape=[jax.ShapeDtypeStruct(*s) for s in outs],
        in_specs=specs,
        out_specs=[pl.BlockSpec(memory_space=pltpu.VMEM)] * len(outs),
        scratch_shapes=list(scratch),
        compiler_params=pltpu.CompilerParams(vmem_limit_bytes=32 * 1024 * 1024),
    )(*args)
    return result[0] if single else result


def swap(value, first):
    pairs = [(i, (i + 1) % NY) for i in range(first, NY, 2)]
    return lax.ppermute(value, "y", pairs + [(j, i) for i, j in pairs])


def local(snapshots, mass_blocks, block_cols, coefficients, lumped):
    nodes = snapshots.shape[0]
    blocks = nodes // BLOCK
    own = jnp.transpose(snapshots, (1, 0, 2))
    tile = jnp.concatenate([own.reshape(3 * nodes, TILE), coefficients.T], axis=0)
    cut = tile.shape[0] // 2

    mass = mass_blocks.reshape(blocks, BPR, BLOCK, BLOCK).transpose(1, 0, 2, 3)
    up, down = [tile], [tile]
    up.append(swap(tile, 0))
    down.append(swap(tile, 1))
    edge = ((REACH, BLOCK, 3 * TILE), F32)
    low, mid, high, weight = call(
        dual_kernel,
        [edge, ((blocks, BLOCK, 3 * TILE), F32), edge, ((1, nodes), F32)],
        block_cols,
        mass,
        own,
        lumped.reshape(1, nodes),
        scratch=[pltpu.VMEM((blocks + 2 * REACH, BLOCK, 3 * TILE), F32)],
        smem=1,
    )
    first, low, high = lax.optimization_barrier((up[1], low, high))
    down.append(swap(first, 1))
    up.append(swap(down[1], 0))
    low, high, down[1] = lax.optimization_barrier((low, high, down[1]))
    from_next = lax.ppermute(low, SPACE, [(i + 1, i) for i in range(NSPACE - 1)])
    from_prev = lax.ppermute(high, SPACE, [(i, i + 1) for i in range(NSPACE - 1)])
    raw = call(first_kernel, ((MODES, 3 * nodes), F32), tile, up[1], down[1])
    second, raw = lax.optimization_barrier((down[2], raw))
    up.append(swap(second, 0))
    down.append(swap(up[2], 1))
    dual = call(join_kernel, ((3 * nodes, 2 * TILE), BF16), mid, from_next, from_prev)

    half_a = swap(down[3][:cut], 0)
    half_b = swap(up[3][cut:], 1)

    near = [0, 1, NY - 1, 2, NY - 2, 3, NY - 3]
    early, raw = call(
        lambda *refs: early_kernel(len(near), *refs),
        [((len(near), TILE, TILE), F32), ((MODES, 3 * nodes), F32)],
        dual,
        raw,
        tile,
        up[1],
        down[1],
        up[2],
        down[2],
        up[3],
        down[3],
    )
    own_slots = ((NSPACE // NC, OWN, TILE), F32)
    far_slots = ((NSPACE // NC + 1, OWN, TILE), F32)
    mine, other, norm, raw = call(
        lambda *refs: late_kernel(near, *refs),
        [own_slots, far_slots, ((SLOT - OWN, TILE), F32), ((3, MODES, nodes), F32)],
        dual,
        early,
        raw,
        weight,
        half_a,
        half_b,
    )
    other = lax.ppermute(other, "core", [(0, 1), (1, 0)])
    slots = call(pair_kernel, ((NSPACE // NC, SLOT, TILE), BF16), mine, other, norm)
    parts = lax.all_to_all(slots, ("x", "z"), split_axis=0, concat_axis=0, tiled=True)
    gram, modes = call(
        lambda *refs: final_kernel(3.0 * nodes * NSPACE, *refs),
        [((OWN, TILE), F32), ((3, MODES, nodes), BF16)],
        parts,
        raw,
    )
    return gram.T, jnp.transpose(modes, (2, 0, 1))


def solution(mesh):
    fine = Mesh(mesh.devices.reshape(NX, NZ, NC, NY), ("x", "z", "core", "y"))
    return jax.shard_map(
        local,
        mesh=fine,
        in_specs=(
            P(SPACE, None, "y"),
            P(SPACE, None, None),
            P(SPACE, None),
            P("y", None),
            P(SPACE),
        ),
        out_specs=(P("y", SPACE), P(SPACE, None, None)),
        check_vma=False,
    )
```

```python
import jax
import jax.numpy as jnp
from jax import lax
from jax.experimental import pallas as pl
from jax.experimental.pallas import tpu as pltpu
from jax.sharding import Mesh, PartitionSpec as P

BLOCK = 64
BPR = 7
REACH = 3
NX, NZ, NC, NY = 4, 8, 2, 8
NSPACE = NX * NZ * NC
MODES = 64
TILE = 128
OWN = 16
SLOT = 24
F32 = jnp.float32
BF16 = jnp.bfloat16
SPACE = ("x", "z", "core")
ALONG = (((0,), (0,)), ((), ()))


def dual_kernel(cols, mass, own, lumped, low, mid, high, weight, acc):
    weight[...] = lumped[...]
    blocks = own.shape[1] // BLOCK
    index = (lax.axis_index("x") * NZ + lax.axis_index("z")) * NC + lax.axis_index("core")
    first = index * blocks - REACH
    acc[...] = jnp.zeros_like(acc)
    for b in range(blocks):
        rows = slice(b * BLOCK, (b + 1) * BLOCK)
        right = jnp.concatenate([own[c, rows, :] for c in range(3)], axis=1)
        left = jnp.concatenate([mass[j, b] for j in range(BPR)], axis=1)
        terms = lax.dot_general(left, right, ALONG, preferred_element_type=F32)
        for j in range(BPR):
            place = cols[b, j] - first
            acc[place] += terms[j * BLOCK : (j + 1) * BLOCK]
    low[...] = acc[:REACH]
    mid[...] = acc[REACH : REACH + blocks]
    high[...] = acc[REACH + blocks :]


def join_kernel(mid, from_next, from_prev, out):
    blocks = mid.shape[0]
    for b in range(blocks):
        value = mid[b]
        if b < REACH:
            value = value + from_prev[b]
        if b >= blocks - REACH:
            value = value + from_next[b - blocks + REACH]
        high = value.astype(BF16)
        rest = (value - high.astype(F32)).astype(BF16)
        for c in range(3):
            rows = slice((c * blocks + b) * BLOCK, (c * blocks + b + 1) * BLOCK)
            lanes = slice(c * TILE, (c + 1) * TILE)
            out[rows, :TILE] = high[:, lanes]
            out[rows, TILE:] = rest[:, lanes]


def gram_product(tile, dual):
    both = lax.dot_general(tile[: dual.shape[0], :], dual, ALONG, preferred_element_type=F32)
    return both[:, :TILE] + both[:, TILE:]


def raw_product(tile):
    rows = tile.shape[0] - MODES
    return lax.dot_general(
        tile[rows:, :], tile[:rows, :], (((1,), (1,)), ((), ())), preferred_element_type=F32
    )


def first_kernel(own, one, two, raw_out):
    raw_out[...] = raw_product(own[...]) + raw_product(one[...]) + raw_product(two[...])


def early_kernel(count, dual, raw_in, *refs):
    tiles, gram, raw_out = refs[:count], refs[count], refs[count + 1]
    raw = raw_in[...]
    for i in range(count):
        tile = tiles[i][...]
        gram[i] = gram_product(tile, dual[...])
        if i >= 3:
            raw = raw + raw_product(tile)
    raw_out[...] = raw


def late_kernel(near, dual, early, raw_in, lumped, half_a, half_b, mine, other, norm_out, raw_out):
    me = lax.axis_index("y")
    nodes = raw_out.shape[2]
    far = jnp.concatenate([half_a[...], half_b[...]], axis=0)
    product = gram_product(far, dual[...])
    raw = raw_in[...] + raw_product(far)
    column = jnp.zeros((MODES, 1), F32)
    for c in range(3):
        part = raw[:, c * nodes : (c + 1) * nodes]
        raw_out[c] = part
        column = column + jnp.sum(lumped[...] * part * part, axis=1, keepdims=True)
    k = lax.broadcasted_iota(jnp.int32, (MODES, TILE), 0)
    lane = lax.broadcasted_iota(jnp.int32, (MODES, TILE), 1)
    row = jnp.sum(jnp.where(lane % MODES == k, column, 0.0), axis=0, keepdims=True)
    norm_out[...] = jnp.broadcast_to(row, (SLOT - OWN, TILE))
    other[NSPACE // NC] = jnp.broadcast_to(row, (OWN, TILE))
    turn = 1 - 2 * lax.rem(me, 2)
    steps = near + [4]
    first = lax.axis_index("core") == 0
    for i, step in enumerate(steps):
        source = lax.rem(me + step * turn + NY, NY)
        part = early[i] if i < len(near) else product
        for o in range(TILE // OWN // NC):
            one = part[2 * o * OWN : (2 * o + 1) * OWN]
            two = part[(2 * o + 1) * OWN : (2 * o + 2) * OWN]
            place = source * (TILE // OWN // NC) + o
            mine[place] = jnp.where(first, one, two)
            other[place] = jnp.where(first, two, one)


def pair_kernel(mine, other, norm_in, out):
    lane = lax.broadcasted_iota(jnp.int32, (SLOT - OWN, TILE), 1)
    row = norm_in[...] + other[NSPACE // NC, : SLOT - OWN, :]
    high = row.astype(BF16)
    rest = (row - high.astype(F32)).astype(BF16)
    norm = jnp.where(lane < MODES, high.astype(F32), rest.astype(F32))
    for i in range(NSPACE // NC):
        total = mine[i] + other[i]
        out[i] = jnp.concatenate([total, norm], axis=0).astype(BF16)


def final_kernel(count, parts, raw, gram, modes):
    total = parts[0].astype(F32)
    for i in range(1, NSPACE // NC):
        total = total + parts[i].astype(F32)
    gram[...] = total[:OWN] * count ** (-0.5)
    row = total[OWN : OWN + 1]
    row = row + pltpu.roll(row, MODES, 1)
    row = lax.rsqrt(row / count + 1e-06)
    k = lax.broadcasted_iota(jnp.int32, (MODES, TILE), 0)
    lane = lax.broadcasted_iota(jnp.int32, (MODES, TILE), 1)
    column = jnp.sum(jnp.where(lane == k, row, 0.0), axis=1, keepdims=True)
    for c in range(3):
        modes[c] = (raw[c] * column).astype(BF16)


def call(kernel, shapes, *args, scratch=(), smem=0):
    specs = [pl.BlockSpec(memory_space=pltpu.SMEM)] * smem
    specs += [pl.BlockSpec(memory_space=pltpu.VMEM)] * (len(args) - smem)
    single = not isinstance(shapes, list)
    outs = [shapes] if single else shapes
    result = pl.pallas_call(
        kernel,
        out_shape=[jax.ShapeDtypeStruct(*s) for s in outs],
        in_specs=specs,
        out_specs=[pl.BlockSpec(memory_space=pltpu.VMEM)] * len(outs),
        scratch_shapes=list(scratch),
        compiler_params=pltpu.CompilerParams(vmem_limit_bytes=32 * 1024 * 1024),
    )(*args)
    return result[0] if single else result


def swap(value, first):
    pairs = [(i, (i + 1) % NY) for i in range(first, NY, 2)]
    return lax.ppermute(value, "y", pairs + [(j, i) for i, j in pairs])


def local(snapshots, mass_blocks, block_cols, coefficients, lumped):
    nodes = snapshots.shape[0]
    blocks = nodes // BLOCK
    own = jnp.transpose(snapshots, (1, 0, 2))
    tile = jnp.concatenate([own.reshape(3 * nodes, TILE), coefficients.T], axis=0)
    cut = tile.shape[0] * 2 // 5

    mass = mass_blocks.reshape(blocks, BPR, BLOCK, BLOCK).transpose(1, 0, 2, 3)
    up, down = [tile], [tile]
    up.append(swap(tile, 0))
    down.append(swap(tile, 1))
    edge = ((REACH, BLOCK, 3 * TILE), F32)
    low, mid, high, weight = call(
        dual_kernel,
        [edge, ((blocks, BLOCK, 3 * TILE), F32), edge, ((1, nodes), F32)],
        block_cols,
        mass,
        own,
        lumped.reshape(1, nodes),
        scratch=[pltpu.VMEM((blocks + 2 * REACH, BLOCK, 3 * TILE), F32)],
        smem=1,
    )
    first, low, high = lax.optimization_barrier((up[1], low, high))
    down.append(swap(first, 1))
    up.append(swap(down[1], 0))
    low, high, down[1] = lax.optimization_barrier((low, high, down[1]))
    from_next = lax.ppermute(low, SPACE, [(i + 1, i) for i in range(NSPACE - 1)])
    from_prev = lax.ppermute(high, SPACE, [(i, i + 1) for i in range(NSPACE - 1)])
    raw = call(first_kernel, ((MODES, 3 * nodes), F32), tile, up[1], down[1])
    second, raw = lax.optimization_barrier((down[2], raw))
    up.append(swap(second, 0))
    down.append(swap(up[2], 1))
    dual = call(join_kernel, ((3 * nodes, 2 * TILE), BF16), mid, from_next, from_prev)

    half_a = swap(down[3][:cut], 0)
    half_b = swap(up[3][cut:], 1)

    near = [0, 1, NY - 1, 2, NY - 2, 3, NY - 3]
    early, raw = call(
        lambda *refs: early_kernel(len(near), *refs),
        [((len(near), TILE, TILE), F32), ((MODES, 3 * nodes), F32)],
        dual,
        raw,
        tile,
        up[1],
        down[1],
        up[2],
        down[2],
        up[3],
        down[3],
    )
    own_slots = ((NSPACE // NC, OWN, TILE), F32)
    far_slots = ((NSPACE // NC + 1, OWN, TILE), F32)
    mine, other, norm, raw = call(
        lambda *refs: late_kernel(near, *refs),
        [own_slots, far_slots, ((SLOT - OWN, TILE), F32), ((3, MODES, nodes), F32)],
        dual,
        early,
        raw,
        weight,
        half_a,
        half_b,
    )
    other = lax.ppermute(other, "core", [(0, 1), (1, 0)])
    slots = call(pair_kernel, ((NSPACE // NC, SLOT, TILE), BF16), mine, other, norm)
    parts = lax.all_to_all(slots, ("x", "z"), split_axis=0, concat_axis=0, tiled=True)
    gram, modes = call(
        lambda *refs: final_kernel(3.0 * nodes * NSPACE, *refs),
        [((OWN, TILE), F32), ((3, MODES, nodes), BF16)],
        parts,
        raw,
    )
    return gram.T, jnp.transpose(modes, (2, 0, 1))


def solution(mesh):
    fine = Mesh(mesh.devices.reshape(NX, NZ, NC, NY), ("x", "z", "core", "y"))
    return jax.shard_map(
        local,
        mesh=fine,
        in_specs=(
            P(SPACE, None, "y"),
            P(SPACE, None, None),
            P(SPACE, None),
            P("y", None),
            P(SPACE),
        ),
        out_specs=(P("y", SPACE), P(SPACE, None, None)),
        check_vma=False,
    )
```
